32 devices in a mesh: section: 4 (over y, core), fsdp: 4 (over z), tp: 2 (over x).
Axes of the slice: x: 2, y: 2, z: 4, core: 2. Of those that a mesh axis runs over, the one named last changes fastest.
Arguments:
- text_tokens: bfloat16 [4096, 8192], P(('section', 'fsdp')), may hold values from -45 to 45
- images: bfloat16 [16, 256, 8192], P('section', None, ('fsdp', 'tp')), may hold values from -45 to 45
- counts: int32 [16], P('section'), may hold values from 1 to 256, as said below
- offsets: int32 [16], P('section'), may hold values from 0 to 4095, as said below
- norm_gain: float32 [8192], replicated, may hold values from 0.25 to 1.75
- value_weight: bfloat16 [8192, 512], P(('fsdp', 'tp'), 'section'), may hold values from -0.0625 to 0.0625
- value_grad: bfloat16 [4096, 512], P(('section', 'fsdp')), may hold values from -6 to 6
Outputs:
- values: bfloat16 [4096, 512], P(('section', 'fsdp'), 'tp')
- visual_grads: bfloat16 [16, 256, 8192], P('section', None, ('fsdp', 'tp'))
The draws below stay inside these ranges and needn't reach their ends.
Inputs may be any that keep to these rules, and one draw needn't show every extreme that they name: `counts`: on every section index some tile has exactly 256 visual tokens. Tile i occupies positions offsets[i] to offsets[i] + counts[i] - 1, all inside one aligned block of 256 positions. The positions of one section index form 4 such blocks. The 4 tiles of one section index go to 4 different section indices, and every block receives exactly one tile.
All inputs are finite; a program needn't handle non-finite values.
Results may differ from the reference program's by a relative error of at most 0.0049.
Values may be sent and summed in bfloat16 or wider, within the bound.
A program may use at most 64 MiB of HBM per device.

```python
import math
import jax
import jax.numpy as jnp
from jax import lax

D = 8192
PMAX = 256
IMAGES = 16
TOK_DEV = 256
TOKENS = 4096
VALUE_WIDTH = 512
N_SECTION = 4
N_FSDP = 4


def rough_rows(key, rows, width):
    subkeys = jax.random.split(key, 3)
    row_factor = jnp.exp(jax.random.uniform(subkeys[0], (rows, 1), minval=math.log(0.3), maxval=math.log(3.0)))
    column_factor = jnp.exp(jax.random.uniform(subkeys[1], (1, width), minval=math.log(0.3), maxval=math.log(3.0)))
    base_draw = jnp.clip(jax.random.normal(subkeys[2], (rows, width)), -5.0, 5.0)
    return jnp.clip(base_draw * row_factor * column_factor, -45.0, 45.0)


def draw_text_tokens(key, part):
    return rough_rows(jax.random.fold_in(key, 21), TOKENS, D).astype(jnp.bfloat16)


def draw_images(key, part):
    return rough_rows(jax.random.fold_in(key, 22), IMAGES * PMAX, D).reshape(IMAGES, PMAX, D).astype(jnp.bfloat16)


def placement_draw(key):
    subkeys = jax.random.split(jax.random.fold_in(key, 7), 5)
    sections = N_SECTION
    grid_shape = (sections, sections)
    counts = jax.random.randint(subkeys[0], grid_shape, 1, PMAX + 1)
    full_image = jax.random.randint(subkeys[1], (sections, 1), 0, sections)
    slot_ids = jnp.arange(sections, dtype=jnp.int32)[None, :]
    counts = jnp.where(slot_ids == full_image, PMAX, counts)
    scores = jax.random.randint(subkeys[2], grid_shape, 0, 1 << 20) * sections + slot_ids
    target = jnp.argsort(scores, axis=-1).astype(jnp.int32)
    scores_two = jax.random.randint(subkeys[3], grid_shape, 0, 1 << 20) * sections + slot_ids
    region_perm = jnp.argsort(scores_two, axis=-1).astype(jnp.int32)
    source = jnp.arange(sections, dtype=jnp.int32)[:, None]
    region = region_perm[target, source]
    first_slot = jax.random.randint(subkeys[4], grid_shape, 0, PMAX - counts + 1)
    offsets = target * (N_FSDP * TOK_DEV) + region * PMAX + first_slot
    return (counts.reshape(-1).astype(jnp.int32), offsets.reshape(-1).astype(jnp.int32))


def draw_counts(key, part):
    return placement_draw(key)[0]


def draw_offsets(key, part):
    return placement_draw(key)[1]


def shard_levels(rng, shape, pieces, low, largest):
    gain, own = 1.0, jax.random.fold_in(rng, 6)
    for dim, parts in pieces:
        draws = jnp.exp(jax.random.uniform(jax.random.fold_in(own, dim), (parts,), jnp.float32, low / len(pieces), largest / len(pieces)))
        gain = gain * jnp.repeat(draws, shape[dim] // parts).reshape([-1 if axis == dim else 1 for axis in range(len(shape))])
    return gain


def centred(key, shape, spread, bound, pieces=(), held_as=jnp.bfloat16):
    entries = spread * jax.random.normal(key, shape, jnp.float32)
    if pieces:
        entries = entries * shard_levels(key, shape, pieces, -0.22, 0.18)
    return jnp.clip(entries, -bound, bound).astype(held_as)


def setup_inputs(seed: int = 0) -> dict:
    keys = jax.random.split(jax.random.key(seed), 8)
    return {
        "text_tokens": draw_text_tokens(jax.random.fold_in(keys[7], 71), 0),
        "images": draw_images(jax.random.fold_in(keys[7], 71), 0),
        "counts": draw_counts(jax.random.fold_in(keys[7], 71), 0),
        "offsets": draw_offsets(jax.random.fold_in(keys[7], 71), 0),
        "norm_gain": jnp.clip(1.0 + 0.15 * jax.random.normal(keys[4], (D,), jnp.float32), 0.25, 1.75),
        "value_weight": centred(keys[5], (D, VALUE_WIDTH), D ** -0.5, 0.0625, ((0, 8), (1, 4))),
        "value_grad": centred(keys[6], (TOKENS, VALUE_WIDTH), 1.0, 6.0, ((0, 16),)),
    }


epsilon = 1e-05

def row_scale(rows):
    values_f = rows.astype(jnp.float32)
    return lax.rsqrt(lax.optimization_barrier(jnp.mean(values_f * values_f, axis=-1, keepdims=True)) + epsilon)

def normalize(rows, norm_gain):
    inv_rms = row_scale(rows)
    return (rows.astype(jnp.float32) * inv_rms * norm_gain).astype(jnp.bfloat16)

def norm_back(rows, inv_rms, norm_gain, grad_normed):
    values_f = rows.astype(jnp.float32)
    weighted = grad_normed * norm_gain
    inner_dot = lax.optimization_barrier(jnp.sum(weighted * values_f, axis=-1, keepdims=True))
    return inv_rms * weighted - values_f * (inv_rms * inv_rms * inv_rms) * inner_dot / rows.shape[-1]

def reference(text_tokens, images, counts, offsets, norm_gain, value_weight, value_grad):
    slot_idx = jnp.arange(PMAX, dtype=jnp.int32)
    is_valid = slot_idx[None, :] < counts[:, None]
    position = jnp.where(is_valid, offsets[:, None] + slot_idx[None, :], TOKENS).reshape(-1).astype(jnp.int32)
    flat_images = images.reshape(-1, D)
    mixed_rows = text_tokens.at[position].set(flat_images, mode='drop')

    def project(row_block):
        normed = normalize(row_block, norm_gain)
        return jnp.dot(normed, value_weight, preferred_element_type=jnp.float32).astype(jnp.bfloat16)
    values = lax.map(project, mixed_rows.reshape(-1, TOK_DEV, D)).reshape(TOKENS, VALUE_WIDTH)
    valid_flat = is_valid.reshape(-1)
    safe_pos = jnp.where(valid_flat, position, 0).astype(jnp.int32)
    slot_grad = jnp.where(valid_flat[:, None], value_grad[safe_pos], jnp.zeros((), jnp.bfloat16))

    def backward(pair):
        rows, grad_rows = pair
        grad_normed = jnp.dot(grad_rows, value_weight.T, preferred_element_type=jnp.float32)
        return norm_back(rows, row_scale(rows), norm_gain, grad_normed).astype(jnp.bfloat16)
    visual_grads = lax.map(backward, (images, slot_grad.reshape(IMAGES, PMAX, VALUE_WIDTH)))
    return (values, visual_grads)
```

```python
import jax
import jax.numpy as jnp
from jax import lax
from jax.sharding import PartitionSpec as P

epsilon = 1e-05
f32 = jnp.float32
bf16 = jnp.bfloat16


def on_device(text_tokens, images, counts, offsets, norm_gain, value_weight, value_grad):
    sections = lax.axis_size("section")
    columns = lax.axis_size("fsdp")
    pairs = lax.axis_size("tp")
    tok_rows, width = text_tokens.shape
    tiles, slots, part = images.shape
    heads = value_grad.shape[1]
    group_rows = columns * tok_rows
    regions = group_rows // slots
    section = lax.axis_index("section")
    column = lax.axis_index("fsdp")
    pair = lax.axis_index("tp")

    meta = lax.all_gather(jnp.stack([offsets, counts]), "section", axis=0)
    all_off, all_cnt = meta[:, 0], meta[:, 1]
    w_own = lax.all_gather(value_weight, "section", axis=1, tiled=True)
    w_all = lax.all_gather(w_own, "fsdp", axis=0, tiled=True)
    grad_group = lax.all_gather(value_grad, "fsdp", axis=0, tiled=True)

    here = (all_off // group_rows) == section
    start_here = jnp.sum(jnp.where(here, all_off - section * group_rows, 0), axis=1)
    count_here = jnp.sum(jnp.where(here, all_cnt, 0), axis=1)
    slot_ids = jnp.arange(slots, dtype=jnp.int32)
    rows_here = jnp.where(
        slot_ids[None, :] < count_here[:, None], start_here[:, None] + slot_ids[None, :], -1
    ).reshape(-1)
    group_ids = jnp.arange(group_rows, dtype=jnp.int32)
    select_here = (rows_here[:, None] == group_ids[None, :]).astype(bf16)
    grad_out = jnp.dot(select_here, grad_group, preferred_element_type=f32).astype(bf16)
    grad_in = lax.all_to_all(
        grad_out.reshape(sections, slots, heads), "section", split_axis=0, concat_axis=0, tiled=True
    )
    target = offsets // group_rows
    route = (target[:, None] == jnp.arange(sections, dtype=jnp.int32)[None, :]).astype(bf16)
    grad_slots = jnp.einsum("kt,tjc->kjc", route, grad_in, preferred_element_type=f32).astype(bf16)
    grad_slots = grad_slots.reshape(tiles * slots, heads)

    flat = images.reshape(tiles * slots, part)
    flat_f = flat.astype(f32)
    square_sum = lax.psum(jnp.sum(flat_f * flat_f, axis=1), ("fsdp", "tp"))
    inv_rms = lax.rsqrt(square_sum / width + epsilon)[:, None]

    own = (column * pairs + pair) * part
    gain_part = lax.dynamic_slice_in_dim(norm_gain, own, part)
    w_gain = (w_own.astype(f32) * gain_part[:, None]).astype(bf16)
    product = jnp.dot(flat, w_gain, preferred_element_type=f32)
    inner = lax.psum(jnp.sum(product * grad_slots.astype(f32), axis=1), ("fsdp", "tp"))[:, None]
    grad_normed = lax.dot_general(
        grad_slots, w_own, (((1,), (1,)), ((), ())), preferred_element_type=f32
    )
    visual_grads = (
        inv_rms * (grad_normed * gain_part) - flat_f * (inv_rms * inv_rms * inv_rms) * inner / width
    ).astype(bf16)
    valid = (slot_ids[None, :] < counts[:, None]).reshape(-1, 1)
    visual_grads = jnp.where(valid, visual_grads, 0).reshape(images.shape)

    scaled = (product * inv_rms).astype(bf16).reshape(tiles, slots, heads)
    out_parts = jnp.einsum("kt,kjc->tjc", route, scaled, preferred_element_type=f32).astype(bf16)
    in_parts = lax.all_to_all(out_parts, "section", split_axis=0, concat_axis=0, tiled=True)
    placed = lax.dot_general(
        select_here,
        in_parts.reshape(sections * slots, heads),
        (((0,), (0,)), ((), ())),
        preferred_element_type=f32,
    ).astype(bf16)
    by_column = lax.all_to_all(
        placed.reshape(columns, tok_rows, heads), "fsdp", split_axis=0, concat_axis=0, tiled=True
    )
    visual_part = jnp.sum(by_column.astype(f32), axis=0)

    row_ids = column * tok_rows + jnp.arange(tok_rows, dtype=jnp.int32)
    covered = jnp.any(rows_here[None, :] == row_ids[:, None], axis=1)[:, None]
    text_f = text_tokens.astype(f32)
    text_rms = lax.rsqrt(jnp.sum(text_f * text_f, axis=1, keepdims=True) / width + epsilon)
    text_own = jnp.concatenate(
        [
            lax.dynamic_slice_in_dim(text_tokens, (f * pairs + pair) * part, part, axis=1)
            for f in range(columns)
        ],
        axis=1,
    )
    gain_own = jnp.concatenate(
        [
            lax.dynamic_slice_in_dim(norm_gain, (f * pairs + pair) * part, part)
            for f in range(columns)
        ]
    )
    w_all_gain = (w_all.astype(f32) * gain_own[:, None]).astype(bf16)
    text_part = jnp.dot(text_own, w_all_gain, preferred_element_type=f32) * text_rms
    part_values = jnp.where(covered, visual_part, text_part)
    values = lax.psum_scatter(part_values, "tp", scatter_dimension=1, tiled=True).astype(bf16)
    return (values, visual_grads)


def solution(mesh):
    placed = (
        P(("section", "fsdp"), None),
        P("section", None, ("fsdp", "tp")),
        P("section"),
        P("section"),
        P(),
        P(("fsdp", "tp"), "section"),
        P(("section", "fsdp"), None),
    )
    return jax.shard_map(
        on_device,
        mesh=mesh,
        in_specs=placed,
        out_specs=(P(("section", "fsdp"), "tp"), P("section", None, ("fsdp", "tp"))),
        check_vma=False,
    )
```

```python
import functools

import jax
import jax.numpy as jnp
from jax import lax
from jax.experimental import pallas as pl
from jax.experimental.pallas import tpu as pltpu
from jax.sharding import PartitionSpec as P

epsilon = 1e-05
f32 = jnp.float32
bf16 = jnp.bfloat16
MESH = pl.DeviceIdType.MESH


def kernel(
    width,
    a_tab,
    b_tab,
    r_tab,
    vg_ref,
    img_ref,
    sq_ref,
    wt_ref,
    grads,
    vis_ref,
    sqt_ref,
    inner_ref,
    wown,
    gath,
    gout,
    gin,
    ghalf,
    prod,
    pout,
    pin,
    psum,
    bout,
    bin_,
    cout,
    cin,
    sqbuf,
    innbuf,
    innown,
    s_vg,
    r_vg,
    s_w,
    r_w,
    s_sq,
    r_sq,
    s_a2,
    r_a2,
    s_a3,
    r_a3,
    s_b1,
    r_b1,
    s_b2,
    r_b2,
    s_b3,
    r_b3,
    s_in,
    r_in,
):
    sections, slots, half = gout.shape
    columns, tok, _ = cin.shape
    pairs = pout.shape[0]
    rows = psum.shape[0]
    tiles = rows // slots
    cols = wt_ref.shape[0]
    me_s, me_f, me_t = (lax.axis_index(n) for n in ("section", "fsdp", "tp"))
    others_s = [lax.rem(me_s + d, sections) for d in range(1, sections)]
    others_f = [lax.rem(me_f + d, columns) for d in range(1, columns)]
    others_t = [lax.rem(me_t + d, pairs) for d in range(1, pairs)]
    group = columns * pairs
    me_g = me_f * pairs + me_t
    others_g = [lax.rem(me_g + d, group) for d in range(1, group)]

    def on_s(s):
        return (s, me_f, me_t)

    def on_f(f):
        return (me_s, f, me_t)

    def on_t(t):
        return (me_s, me_f, t)

    def on_g(g):
        return (me_s, g // pairs, lax.rem(g, pairs))

    def copy(src, dst, s, r, dev):
        return pltpu.make_async_remote_copy(
            src_ref=src, dst_ref=dst, send_sem=s, recv_sem=r, device_id=dev, device_id_type=MESH
        )

    barrier = pltpu.get_barrier_semaphore()
    peers = [on_s(s) for s in others_s] + [on_g(g) for g in others_g]
    for dev in peers:
        pl.semaphore_signal(barrier, inc=1, device_id=dev, device_id_type=MESH)
    pl.semaphore_wait(barrier, len(peers))

    def slot(i, n):
        return pl.ds(pl.multiple_of(i * n, n), n)

    sent = []

    def send(src, dst, s, r, dev):
        c = copy(src, dst, s, r, dev)
        c.start()
        sent.append(c)

    for g in others_g:
        send(sq_ref, sqbuf.at[me_g], s_sq.at[g], r_sq.at[me_g], on_g(g))
    for s in others_s:
        send(wt_ref, wown.at[slot(me_s, cols)], s_w.at[s], r_w.at[me_s], on_s(s))
    for f in others_f:
        send(vg_ref, gath.at[slot(me_f, tok)], s_vg.at[f], r_vg.at[me_f], on_f(f))
    gath[slot(me_f, tok)] = vg_ref[...]
    wown[slot(me_s, cols)] = wt_ref[...]
    sqbuf[me_g] = sq_ref[...]

    def one_hot(n, m, start, lo, hi):
        r = lax.broadcasted_iota(jnp.int32, (n, m), 0)
        c = lax.broadcasted_iota(jnp.int32, (n, m), 1)
        hit = (c - r == start) & (r >= lo) & (r < hi)
        return jnp.where(hit, 1.0, 0.0).astype(bf16)

    def pick(n, start, lo, hi, ref):
        m = ref.shape[0]
        return jnp.dot(
            one_hot(n, m, start, lo, hi), ref[...], preferred_element_type=f32
        ).astype(bf16)

    for f in others_f:
        copy(vg_ref, gath.at[slot(f, tok)], s_vg.at[f], r_vg.at[f], on_f(f)).wait_recv()
    for s in others_s + [me_s]:
        block = pick(slots, a_tab[0, s], 0, a_tab[1, s], gath)
        if s is me_s:
            gin[slot(s, slots)] = block
        else:
            gout[s] = block
            send(gout.at[s], gin.at[slot(me_s, slots)], s_a2.at[s], r_a2.at[me_s], on_s(s))

    eye = lax.broadcasted_iota(jnp.int32, (128, 128), 0) == lax.broadcasted_iota(
        jnp.int32, (128, 128), 1
    )
    for g in others_g:
        copy(sq_ref, sqbuf.at[g], s_sq.at[g], r_sq.at[g], on_g(g)).wait_recv()
    total = jnp.sum(sqbuf[...], axis=0)
    sqt_ref[...] = total
    for s in others_s:
        copy(wt_ref, wown.at[slot(s, cols)], s_w.at[s], r_w.at[s], on_s(s)).wait_recv()

    def project(k, carry):
        at = slot(k, slots)
        p = lax.dot_general(
            img_ref[at], wown[...], (((1,), (1,)), ((), ())), preferred_element_type=f32
        )
        prod[at] = p
        for j in range(0, slots, 128):
            at_j = pl.ds(pl.multiple_of(k * slots + j, 128), 128)
            inv = lax.rsqrt(sqt_ref[:, at_j] / width + epsilon)
            inv = jnp.sum(jnp.where(eye, inv, 0.0), axis=1, keepdims=True)
            part = (p[j : j + 128] * inv).astype(bf16)
            for h in range(pairs):
                pout[h, at_j] = part[:, h * half : (h + 1) * half]
        return carry

    lax.fori_loop(0, tiles, project, 0)
    for t in others_t:
        send(pout.at[t], pin.at[me_t], s_b1.at[t], r_b1.at[me_t], on_t(t))
    pin[me_t] = pout[me_t]

    for s in others_s:
        copy(gout.at[s], gin.at[slot(s, slots)], s_a2.at[s], r_a2.at[s], on_s(s)).wait_recv()

    def order(k, carry):
        ghalf[slot(k, slots)] = pick(slots, r_tab[0, k], 0, slots, gin)
        return carry

    lax.fori_loop(0, tiles, order, 0)
    for t in others_t:
        send(ghalf, grads.at[me_t], s_a3.at[t], r_a3.at[me_t], on_t(t))
    grads[me_t] = ghalf[...]

    for t in others_t:
        copy(pout.at[t], pin.at[t], s_b1.at[t], r_b1.at[t], on_t(t)).wait_recv()
    acc = pin[0].astype(f32)
    for t in range(1, pairs):
        acc = acc + pin[t].astype(f32)
    psum[...] = acc.astype(bf16)
    for s in others_s + [me_s]:
        block = pick(slots, r_tab[1, s], 0, slots, psum)
        if s is me_s:
            bin_[slot(s, slots)] = block
        else:
            bout[s] = block
            send(bout.at[s], bin_.at[slot(me_s, slots)], s_b2.at[s], r_b2.at[me_s], on_s(s))

    for t in others_t:
        copy(ghalf, grads.at[t], s_a3.at[t], r_a3.at[t], on_t(t)).wait_recv()

    def dots(k, carry):
        at = pl.ds(pl.multiple_of(k * 128, 128), 128)
        s = jnp.zeros((128, half), f32)
        for h in range(pairs):
            s = s + prod[at, h * half : (h + 1) * half] * grads[h, at].astype(f32)
        col = jnp.sum(s, axis=1, keepdims=True)
        innown[:, at] = jnp.sum(jnp.where(eye, col, 0.0), axis=0, keepdims=True)
        return carry

    lax.fori_loop(0, rows // 128, dots, 0)
    for g in others_g:
        send(innown, innbuf.at[me_g], s_in.at[g], r_in.at[me_g], on_g(g))
    innbuf[me_g] = innown[...]

    for s in others_s:
        copy(bout.at[s], bin_.at[slot(s, slots)], s_b2.at[s], r_b2.at[s], on_s(s)).wait_recv()
    for f in others_f + [me_f]:
        base = lax.rem(f * tok, slots)
        r = (f * tok) // slots
        block = pick(tok, b_tab[0, r] + base, b_tab[1, r] - base, b_tab[2, r] - base, bin_)
        if f is me_f:
            cin[f] = block
        else:
            cout[f] = block
            send(cout.at[f], cin.at[me_f], s_b3.at[f], r_b3.at[me_f], on_f(f))
    for g in others_g:
        copy(innown, innbuf.at[g], s_in.at[g], r_in.at[g], on_g(g)).wait_recv()
    inner_ref[...] = jnp.sum(innbuf[...], axis=0)
    for f in others_f:
        copy(cout.at[f], cin.at[f], s_b3.at[f], r_b3.at[f], on_f(f)).wait_recv()
    acc = cin[0].astype(f32)
    for f in range(1, columns):
        acc = acc + cin[f].astype(f32)
    vis_ref[...] = acc
    for c in sent:
        c.wait_send()


def exchange(a_tab, b_tab, r_tab, vg_half, img_gain, squares, w_t, dims, width):
    sections, columns, pairs = dims
    tok, half = vg_half.shape
    rows, part = img_gain.shape
    slots = rows // r_tab.shape[1]
    heads = half * pairs
    group = columns * pairs
    vmem = pl.BlockSpec(memory_space=pltpu.VMEM)
    smem = pl.BlockSpec(memory_space=pltpu.SMEM)
    sems = []
    for n in (columns, sections, group, sections, pairs, pairs, sections, columns, group):
        sems += [pltpu.SemaphoreType.DMA((n,))] * 2
    return pl.pallas_call(
        functools.partial(kernel, width),
        out_shape=(
            jax.ShapeDtypeStruct((pairs, rows, half), bf16),
            jax.ShapeDtypeStruct((tok, half), f32),
            jax.ShapeDtypeStruct((1, rows), f32),
            jax.ShapeDtypeStruct((1, rows), f32),
            jax.ShapeDtypeStruct((heads, part), bf16),
        ),
        in_specs=[smem] * 3 + [vmem] * 4,
        out_specs=(vmem,) * 5,
        scratch_shapes=[
            pltpu.VMEM((columns * tok, half), bf16),
            pltpu.VMEM((sections, slots, half), bf16),
            pltpu.VMEM((sections * slots, half), bf16),
            pltpu.VMEM((rows, half), bf16),
            pltpu.VMEM((rows, heads), f32),
            pltpu.VMEM((pairs, rows, half), bf16),
            pltpu.VMEM((pairs, rows, half), bf16),
            pltpu.VMEM((rows, half), bf16),
            pltpu.VMEM((sections, slots, half), bf16),
            pltpu.VMEM((sections * slots, half), bf16),
            pltpu.VMEM((columns, tok, half), bf16),
            pltpu.VMEM((columns, tok, half), bf16),
            pltpu.VMEM((group, 1, rows), f32),
            pltpu.VMEM((group, 1, rows), f32),
            pltpu.VMEM((1, rows), f32),
        ]
        + sems,
        compiler_params=pltpu.CompilerParams(
            collective_id=0, has_side_effects=True, vmem_limit_bytes=56 * 1024 * 1024
        ),
        cost_estimate=pl.CostEstimate(
            flops=40 * rows * part * heads, bytes_accessed=64 * rows * heads, transcendentals=0
        ),
    )(a_tab, b_tab, r_tab, vg_half, img_gain, squares, w_t)


def on_device(text_tokens, images, counts, offsets, norm_gain, value_weight, value_grad):
    sections = lax.axis_size("section")
    columns = lax.axis_size("fsdp")
    pairs = lax.axis_size("tp")
    tok_rows, width = text_tokens.shape
    tiles, slots, part = images.shape
    heads = value_grad.shape[1]
    half = heads // pairs
    group_rows = columns * tok_rows
    regions = group_rows // slots
    section = lax.axis_index("section")
    column = lax.axis_index("fsdp")
    pair = lax.axis_index("tp")

    meta = lax.all_gather(jnp.stack([offsets, counts]), "section", axis=0)
    all_off, all_cnt = meta[:, 0], meta[:, 1]
    w_rows = lax.all_gather(value_weight, "fsdp", axis=0, tiled=True)
    w_all = lax.all_gather(w_rows, "section", axis=1, tiled=True)

    here = (all_off // group_rows) == section
    start_here = jnp.sum(jnp.where(here, all_off - section * group_rows, 0), axis=1)
    count_here = jnp.sum(jnp.where(here, all_cnt, 0), axis=1)
    a_tab = jnp.stack([start_here, count_here])
    region_here = start_here // slots
    first_here = start_here % slots
    source_ids = jnp.arange(sections, dtype=jnp.int32)
    region_ids = jnp.arange(regions, dtype=jnp.int32)
    holds = region_here[None, :] == region_ids[:, None]
    by_region = jnp.stack([source_ids * slots - first_here, first_here, first_here + count_here])
    b_tab = jnp.sum(jnp.where(holds[None], by_region[:, None, :], 0), axis=2)
    target = offsets // group_rows
    tile_ids = jnp.arange(tiles, dtype=jnp.int32)
    inverse = jnp.sum(
        jnp.where(target[None, :] == source_ids[:, None], tile_ids[None, :], 0), axis=1
    )
    r_tab = jnp.stack([target, inverse]) * slots

    own = (column * pairs + pair) * part
    gain_part = lax.dynamic_slice_in_dim(norm_gain, own, part)
    flat = images.reshape(tiles * slots, part)
    flat_f = flat.astype(f32)
    img_gain = (flat_f * gain_part).astype(bf16)
    squares = jnp.sum(flat_f * flat_f, axis=1)[None, :]
    vg_half = lax.dynamic_slice_in_dim(value_grad, pair * half, half, axis=1)
    grads, visual, square_sum, inner, w_own_t = exchange(
        a_tab,
        b_tab,
        r_tab,
        vg_half,
        img_gain,
        squares,
        value_weight.T,
        (sections, columns, pairs),
        width,
    )
    square_sum = square_sum.reshape(-1, 1)
    inner = inner.reshape(-1, 1)
    inv_rms = lax.rsqrt(square_sum / width + epsilon)
    grad_normed = sum(
        jnp.dot(grads[h], w_own_t[h * half : (h + 1) * half], preferred_element_type=f32)
        for h in range(pairs)
    )
    visual_grads = (
        inv_rms * (grad_normed * gain_part) - flat_f * (inv_rms * inv_rms * inv_rms) * inner / width
    ).astype(bf16)
    slot_ids = jnp.arange(slots, dtype=jnp.int32)
    valid = (slot_ids[None, :] < counts[:, None]).reshape(-1, 1)
    visual_grads = jnp.where(valid, visual_grads, 0).reshape(images.shape)

    first_row = column * tok_rows
    local = first_row % slots + jnp.arange(tok_rows, dtype=jnp.int32)
    bounds = lax.dynamic_index_in_dim(b_tab, first_row // slots, 1, keepdims=False)
    covered = ((local >= bounds[1]) & (local < bounds[2]))[:, None]
    text_f = text_tokens.astype(f32)
    text_rms = lax.rsqrt(jnp.sum(text_f * text_f, axis=1, keepdims=True) / width + epsilon)
    text_own = jnp.concatenate(
        [
            lax.dynamic_slice_in_dim(text_tokens, (f * pairs + pair) * part, part, axis=1)
            for f in range(columns)
        ],
        axis=1,
    )
    gain_own = jnp.concatenate(
        [
            lax.dynamic_slice_in_dim(norm_gain, (f * pairs + pair) * part, part)
            for f in range(columns)
        ]
    )
    text_gain = (text_own.astype(f32) * gain_own).astype(bf16)
    text_part = jnp.dot(text_gain, w_all, preferred_element_type=f32) * text_rms
    text_values = lax.psum_scatter(text_part, "tp", scatter_dimension=1, tiled=True)
    values = jnp.where(covered, visual, text_values).astype(bf16)
    return (values, visual_grads)


def solution(mesh):
    placed = (
        P(("section", "fsdp"), None),
        P("section", None, ("fsdp", "tp")),
        P("section"),
        P("section"),
        P(),
        P(("fsdp", "tp"), "section"),
        P(("section", "fsdp"), None),
    )
    return jax.shard_map(
        on_device,
        mesh=mesh,
        in_specs=placed,
        out_specs=(P(("section", "fsdp"), "tp"), P("section", None, ("fsdp", "tp"))),
        check_vma=False,
    )
```

```python
import functools

import jax
import jax.numpy as jnp
from jax import lax
from jax.experimental import pallas as pl
from jax.experimental.pallas import tpu as pltpu
from jax.sharding import PartitionSpec as P

epsilon = 1e-05
f32 = jnp.float32
bf16 = jnp.bfloat16
MESH = pl.DeviceIdType.MESH


def kernel(
    width,
    a_tab,
    b_tab,
    r_tab,
    vg_ref,
    img_ref,
    sq_ref,
    wt_ref,
    grads,
    vis_ref,
    sqt_ref,
    inner_ref,
    wown,
    gath,
    gout,
    gin,
    ghalf,
    prod,
    pout,
    pin,
    psum,
    bout,
    bin_,
    cout,
    cin,
    sqbuf,
    innbuf,
    innown,
    s_vg,
    r_vg,
    s_w,
    r_w,
    s_sq,
    r_sq,
    s_a2,
    r_a2,
    s_a3,
    r_a3,
    s_b1,
    r_b1,
    s_b2,
    r_b2,
    s_b3,
    r_b3,
    s_in,
    r_in,
):
    sections, slots, half = gout.shape
    columns, tok, _ = cin.shape
    pairs = pout.shape[0]
    rows = psum.shape[0]
    tiles = rows // slots
    cols = wt_ref.shape[0]
    me_s, me_f, me_t = (lax.axis_index(n) for n in ("section", "fsdp", "tp"))
    others_s = [lax.rem(me_s + d, sections) for d in range(1, sections)]
    others_f = [lax.rem(me_f + d, columns) for d in range(1, columns)]
    others_t = [lax.rem(me_t + d, pairs) for d in range(1, pairs)]
    group = columns * pairs
    me_g = me_f * pairs + me_t
    others_g = [lax.rem(me_g + d, group) for d in range(1, group)]

    def on_s(s):
        return (s, me_f, me_t)

    def on_f(f):
        return (me_s, f, me_t)

    def on_t(t):
        return (me_s, me_f, t)

    def on_g(g):
        return (me_s, g // pairs, lax.rem(g, pairs))

    def copy(src, dst, s, r, dev):
        return pltpu.make_async_remote_copy(
            src_ref=src, dst_ref=dst, send_sem=s, recv_sem=r, device_id=dev, device_id_type=MESH
        )

    barrier = pltpu.get_barrier_semaphore()
    peers = [on_s(s) for s in others_s] + [on_g(g) for g in others_g]
    for dev in peers:
        pl.semaphore_signal(barrier, inc=1, device_id=dev, device_id_type=MESH)
    pl.semaphore_wait(barrier, len(peers))

    def slot(i, n):
        return pl.ds(pl.multiple_of(i * n, n), n)

    sent = []

    def send(src, dst, s, r, dev):
        c = copy(src, dst, s, r, dev)
        c.start()
        sent.append(c)

    for s in others_s:
        send(wt_ref, wown.at[slot(me_s, cols)], s_w.at[s], r_w.at[me_s], on_s(s))
    for g in others_g:
        send(sq_ref, sqbuf.at[me_g], s_sq.at[g], r_sq.at[me_g], on_g(g))
    for f in others_f:
        send(vg_ref, gath.at[slot(me_f, tok)], s_vg.at[f], r_vg.at[me_f], on_f(f))
    gath[slot(me_f, tok)] = vg_ref[...]
    wown[slot(me_s, cols)] = wt_ref[...]
    sqbuf[me_g] = sq_ref[...]

    def one_hot(n, m, start, lo, hi):
        r = lax.broadcasted_iota(jnp.int32, (n, m), 0)
        c = lax.broadcasted_iota(jnp.int32, (n, m), 1)
        hit = (c - r == start) & (r >= lo) & (r < hi)
        return jnp.where(hit, 1.0, 0.0).astype(bf16)

    def pick(n, start, lo, hi, ref):
        m = ref.shape[0]
        return jnp.dot(
            one_hot(n, m, start, lo, hi), ref[...], preferred_element_type=f32
        ).astype(bf16)

    eye = lax.broadcasted_iota(jnp.int32, (128, 128), 0) == lax.broadcasted_iota(
        jnp.int32, (128, 128), 1
    )
    for g in others_g:
        copy(sq_ref, sqbuf.at[g], s_sq.at[g], r_sq.at[g], on_g(g)).wait_recv()
    total = jnp.sum(sqbuf[...], axis=0)
    sqt_ref[...] = total
    for s in others_s:
        copy(wt_ref, wown.at[slot(s, cols)], s_w.at[s], r_w.at[s], on_s(s)).wait_recv()

    def project(k, carry):
        at = slot(k, slots)
        p = lax.dot_general(
            img_ref[at], wown[...], (((1,), (1,)), ((), ())), preferred_element_type=f32
        )
        prod[at] = p
        for j in range(0, slots, 128):
            at_j = pl.ds(pl.multiple_of(k * slots + j, 128), 128)
            inv = lax.rsqrt(sqt_ref[:, at_j] / width + epsilon)
            inv = jnp.sum(jnp.where(eye, inv, 0.0), axis=1, keepdims=True)
            part = (p[j : j + 128] * inv).astype(bf16)
            for h in range(pairs):
                pout[h, at_j] = part[:, h * half : (h + 1) * half]
        for t in others_t:
            tile_copy(t, me_t, k).start()
        return carry

    def tile_copy(t, source, k):
        at = slot(k, slots)
        return copy(
            pout.at[t, at], pin.at[source, at], s_b1.at[t, k], r_b1.at[source, k], on_t(t)
        )

    lax.fori_loop(0, tiles, project, 0)
    pin[me_t] = pout[me_t]

    for f in others_f:
        copy(vg_ref, gath.at[slot(f, tok)], s_vg.at[f], r_vg.at[f], on_f(f)).wait_recv()
    for s in others_s + [me_s]:
        block = pick(slots, a_tab[0, s], 0, a_tab[1, s], gath)
        if s is me_s:
            gin[slot(s, slots)] = block
        else:
            gout[s] = block
            send(gout.at[s], gin.at[slot(me_s, slots)], s_a2.at[s], r_a2.at[me_s], on_s(s))

    for s in others_s:
        copy(gout.at[s], gin.at[slot(s, slots)], s_a2.at[s], r_a2.at[s], on_s(s)).wait_recv()

    def order(k, carry):
        ghalf[slot(k, slots)] = pick(slots, r_tab[0, k], 0, slots, gin)
        return carry

    lax.fori_loop(0, tiles, order, 0)
    for t in others_t:
        send(ghalf, grads.at[me_t], s_a3.at[t], r_a3.at[me_t], on_t(t))
    grads[me_t] = ghalf[...]

    def arrived(k, carry):
        for t in others_t:
            tile_copy(t, t, k).wait_recv()
        return carry

    lax.fori_loop(0, tiles, arrived, 0)
    acc = pin[0].astype(f32)
    for t in range(1, pairs):
        acc = acc + pin[t].astype(f32)
    psum[...] = acc.astype(bf16)
    for s in others_s + [me_s]:
        block = pick(slots, r_tab[1, s], 0, slots, psum)
        if s is me_s:
            bin_[slot(s, slots)] = block
        else:
            bout[s] = block
            send(bout.at[s], bin_.at[slot(me_s, slots)], s_b2.at[s], r_b2.at[me_s], on_s(s))

    for t in others_t:
        copy(ghalf, grads.at[t], s_a3.at[t], r_a3.at[t], on_t(t)).wait_recv()

    def dots(k, carry):
        at = pl.ds(pl.multiple_of(k * 128, 128), 128)
        s = jnp.zeros((128, half), f32)
        for h in range(pairs):
            s = s + prod[at, h * half : (h + 1) * half] * grads[h, at].astype(f32)
        col = jnp.sum(s, axis=1, keepdims=True)
        innown[:, at] = jnp.sum(jnp.where(eye, col, 0.0), axis=0, keepdims=True)
        return carry

    lax.fori_loop(0, rows // 128, dots, 0)
    for g in others_g:
        send(innown, innbuf.at[me_g], s_in.at[g], r_in.at[me_g], on_g(g))
    innbuf[me_g] = innown[...]

    for s in others_s:
        copy(bout.at[s], bin_.at[slot(s, slots)], s_b2.at[s], r_b2.at[s], on_s(s)).wait_recv()
    for f in others_f + [me_f]:
        base = lax.rem(f * tok, slots)
        r = (f * tok) // slots
        block = pick(tok, b_tab[0, r] + base, b_tab[1, r] - base, b_tab[2, r] - base, bin_)
        if f is me_f:
            cin[f] = block
        else:
            cout[f] = block
            send(cout.at[f], cin.at[me_f], s_b3.at[f], r_b3.at[me_f], on_f(f))
    for g in others_g:
        copy(innown, innbuf.at[g], s_in.at[g], r_in.at[g], on_g(g)).wait_recv()
    inner_ref[...] = jnp.sum(innbuf[...], axis=0)
    for f in others_f:
        copy(cout.at[f], cin.at[f], s_b3.at[f], r_b3.at[f], on_f(f)).wait_recv()
    acc = cin[0].astype(f32)
    for f in range(1, columns):
        acc = acc + cin[f].astype(f32)
    vis_ref[...] = acc
    for c in sent:
        c.wait_send()

    def left(k, carry):
        for t in others_t:
            tile_copy(t, me_t, k).wait_send()
        return carry

    lax.fori_loop(0, tiles, left, 0)


def exchange(a_tab, b_tab, r_tab, vg_half, img_gain, squares, w_t, dims, width):
    sections, columns, pairs = dims
    tok, half = vg_half.shape
    rows, part = img_gain.shape
    slots = rows // r_tab.shape[1]
    heads = half * pairs
    group = columns * pairs
    vmem = pl.BlockSpec(memory_space=pltpu.VMEM)
    smem = pl.BlockSpec(memory_space=pltpu.SMEM)
    sems = []
    tiles = rows // slots
    for n in (columns, sections, group, sections, pairs, (pairs, tiles), sections, columns, group):
        sems += [pltpu.SemaphoreType.DMA(n if isinstance(n, tuple) else (n,))] * 2
    return pl.pallas_call(
        functools.partial(kernel, width),
        out_shape=(
            jax.ShapeDtypeStruct((pairs, rows, half), bf16),
            jax.ShapeDtypeStruct((tok, half), f32),
            jax.ShapeDtypeStruct((1, rows), f32),
            jax.ShapeDtypeStruct((1, rows), f32),
            jax.ShapeDtypeStruct((heads, part), bf16),
        ),
        in_specs=[smem] * 3 + [vmem] * 4,
        out_specs=(vmem,) * 5,
        scratch_shapes=[
            pltpu.VMEM((columns * tok, half), bf16),
            pltpu.VMEM((sections, slots, half), bf16),
            pltpu.VMEM((sections * slots, half), bf16),
            pltpu.VMEM((rows, half), bf16),
            pltpu.VMEM((rows, heads), f32),
            pltpu.VMEM((pairs, rows, half), bf16),
            pltpu.VMEM((pairs, rows, half), bf16),
            pltpu.VMEM((rows, half), bf16),
            pltpu.VMEM((sections, slots, half), bf16),
            pltpu.VMEM((sections * slots, half), bf16),
            pltpu.VMEM((columns, tok, half), bf16),
            pltpu.VMEM((columns, tok, half), bf16),
            pltpu.VMEM((group, 1, rows), f32),
            pltpu.VMEM((group, 1, rows), f32),
            pltpu.VMEM((1, rows), f32),
        ]
        + sems,
        compiler_params=pltpu.CompilerParams(
            collective_id=0, has_side_effects=True, vmem_limit_bytes=56 * 1024 * 1024
        ),
        cost_estimate=pl.CostEstimate(
            flops=40 * rows * part * heads, bytes_accessed=64 * rows * heads, transcendentals=0
        ),
    )(a_tab, b_tab, r_tab, vg_half, img_gain, squares, w_t)


def on_device(text_tokens, images, counts, offsets, norm_gain, value_weight, value_grad):
    sections = lax.axis_size("section")
    columns = lax.axis_size("fsdp")
    pairs = lax.axis_size("tp")
    tok_rows, width = text_tokens.shape
    tiles, slots, part = images.shape
    heads = value_grad.shape[1]
    half = heads // pairs
    group_rows = columns * tok_rows
    regions = group_rows // slots
    section = lax.axis_index("section")
    column = lax.axis_index("fsdp")
    pair = lax.axis_index("tp")

    meta = lax.all_gather(jnp.stack([offsets, counts]), "section", axis=0)
    all_off, all_cnt = meta[:, 0], meta[:, 1]
    w_all = lax.all_gather(value_weight, ("section", "fsdp"), axis=0, tiled=True)
    w_all = w_all.reshape(sections, columns * part, -1)

    here = (all_off // group_rows) == section
    start_here = jnp.sum(jnp.where(here, all_off - section * group_rows, 0), axis=1)
    count_here = jnp.sum(jnp.where(here, all_cnt, 0), axis=1)
    a_tab = jnp.stack([start_here, count_here])
    region_here = start_here // slots
    first_here = start_here % slots
    source_ids = jnp.arange(sections, dtype=jnp.int32)
    region_ids = jnp.arange(regions, dtype=jnp.int32)
    holds = region_here[None, :] == region_ids[:, None]
    by_region = jnp.stack([source_ids * slots - first_here, first_here, first_here + count_here])
    b_tab = jnp.sum(jnp.where(holds[None], by_region[:, None, :], 0), axis=2)
    target = offsets // group_rows
    tile_ids = jnp.arange(tiles, dtype=jnp.int32)
    inverse = jnp.sum(
        jnp.where(target[None, :] == source_ids[:, None], tile_ids[None, :], 0), axis=1
    )
    r_tab = jnp.stack([target, inverse]) * slots

    own = (column * pairs + pair) * part
    gain_part = lax.dynamic_slice_in_dim(norm_gain, own, part)
    flat = images.reshape(tiles * slots, part)
    flat_f = flat.astype(f32)
    img_gain = (flat_f * gain_part).astype(bf16)
    squares = jnp.sum(flat_f * flat_f, axis=1)[None, :]
    vg_half = lax.dynamic_slice_in_dim(value_grad, pair * half, half, axis=1)
    grads, visual, square_sum, inner, w_own_t = exchange(
        a_tab,
        b_tab,
        r_tab,
        vg_half,
        img_gain,
        squares,
        value_weight.T,
        (sections, columns, pairs),
        width,
    )
    first_row = column * tok_rows
    local = first_row % slots + jnp.arange(tok_rows, dtype=jnp.int32)
    bounds = lax.dynamic_index_in_dim(b_tab, first_row // slots, 1, keepdims=False)
    covered = ((local >= bounds[1]) & (local < bounds[2]))[:, None]
    text_f = text_tokens.astype(f32)
    text_rms = lax.rsqrt(jnp.sum(text_f * text_f, axis=1, keepdims=True) / width + epsilon)
    text_own = jnp.concatenate(
        [
            lax.dynamic_slice_in_dim(text_tokens, (f * pairs + pair) * part, part, axis=1)
            for f in range(columns)
        ],
        axis=1,
    )
    gain_own = jnp.concatenate(
        [
            lax.dynamic_slice_in_dim(norm_gain, (f * pairs + pair) * part, part)
            for f in range(columns)
        ]
    )
    text_gain = (text_own.astype(f32) * gain_own).astype(bf16)
    text_part = text_rms * jnp.concatenate(
        [jnp.dot(text_gain, w_all[s], preferred_element_type=f32) for s in range(sections)], axis=1
    )
    grads, text_part = lax.optimization_barrier((grads, text_part))
    text_values = lax.psum_scatter(text_part, "tp", scatter_dimension=1, tiled=True)
    square_sum = square_sum.reshape(-1, 1)
    inner = inner.reshape(-1, 1)
    inv_rms = lax.rsqrt(square_sum / width + epsilon)
    grad_normed = sum(
        jnp.dot(grads[h], w_own_t[h * half : (h + 1) * half], preferred_element_type=f32)
        for h in range(pairs)
    )
    visual_grads = (
        inv_rms * (grad_normed * gain_part) - flat_f * (inv_rms * inv_rms * inv_rms) * inner / width
    ).astype(bf16)
    slot_ids = jnp.arange(slots, dtype=jnp.int32)
    valid = (slot_ids[None, :] < counts[:, None]).reshape(-1, 1)
    visual_grads = jnp.where(valid, visual_grads, 0).reshape(images.shape)

    values = jnp.where(covered, visual, text_values).astype(bf16)
    return (values, visual_grads)


def solution(mesh):
    placed = (
        P(("section", "fsdp"), None),
        P("section", None, ("fsdp", "tp")),
        P("section"),
        P("section"),
        P(),
        P(("fsdp", "tp"), "section"),
        P(("section", "fsdp"), None),
    )
    return jax.shard_map(
        on_device,
        mesh=mesh,
        in_specs=placed,
        out_specs=(P(("section", "fsdp"), "tp"), P("section", None, ("fsdp", "tp"))),
        check_vma=False,
    )
```

```python
import functools

import jax
import jax.numpy as jnp
from jax import lax
from jax.experimental import pallas as pl
from jax.experimental.pallas import tpu as pltpu
from jax.sharding import PartitionSpec as P

epsilon = 1e-05
f32 = jnp.float32
bf16 = jnp.bfloat16
MESH = pl.DeviceIdType.MESH


def kernel(
    width,
    a_tab,
    b_tab,
    r_tab,
    vg_ref,
    img_ref,
    sq_ref,
    wt_ref,
    grads,
    vis_ref,
    sqt_ref,
    inner_ref,
    wown,
    gath,
    gout,
    gin,
    ghalf,
    prod,
    pout,
    pin,
    psum,
    bout,
    bin_,
    cout,
    cin,
    sqbuf,
    innbuf,
    innown,
    s_vg,
    r_vg,
    s_w,
    r_w,
    s_sq,
    r_sq,
    s_a2,
    r_a2,
    s_a3,
    r_a3,
    s_b1,
    r_b1,
    s_b2,
    r_b2,
    s_b3,
    r_b3,
    s_in,
    r_in,
):
    sections, slots, half = gout.shape
    columns, tok, _ = cin.shape
    pairs = pout.shape[0]
    rows = psum.shape[0]
    tiles = rows // slots
    cols = wt_ref.shape[0]
    me_s, me_f, me_t = (lax.axis_index(n) for n in ("section", "fsdp", "tp"))
    others_s = [lax.rem(me_s + d, sections) for d in range(1, sections)]
    others_f = [lax.rem(me_f + d, columns) for d in range(1, columns)]
    others_t = [lax.rem(me_t + d, pairs) for d in range(1, pairs)]
    group = columns * pairs
    me_g = me_f * pairs + me_t
    others_g = [lax.rem(me_g + d, group) for d in range(1, group)]

    def on_s(s):
        return (s, me_f, me_t)

    def on_f(f):
        return (me_s, f, me_t)

    def on_t(t):
        return (me_s, me_f, t)

    def on_g(g):
        return (me_s, g // pairs, lax.rem(g, pairs))

    def copy(src, dst, s, r, dev):
        return pltpu.make_async_remote_copy(
            src_ref=src, dst_ref=dst, send_sem=s, recv_sem=r, device_id=dev, device_id_type=MESH
        )

    barrier = pltpu.get_barrier_semaphore()
    peers = [on_s(s) for s in others_s] + [on_g(g) for g in others_g]
    for dev in peers:
        pl.semaphore_signal(barrier, inc=1, device_id=dev, device_id_type=MESH)
    pl.semaphore_wait(barrier, len(peers))

    def slot(i, n):
        return pl.ds(pl.multiple_of(i * n, n), n)

    sent = []

    def send(src, dst, s, r, dev):
        c = copy(src, dst, s, r, dev)
        c.start()
        sent.append(c)

    for s in others_s:
        send(wt_ref, wown.at[slot(me_s, cols)], s_w.at[s], r_w.at[me_s], on_s(s))
    for g in others_g:
        send(sq_ref, sqbuf.at[me_g], s_sq.at[g], r_sq.at[me_g], on_g(g))
    for f in others_f:
        send(vg_ref, gath.at[slot(me_f, tok)], s_vg.at[f], r_vg.at[me_f], on_f(f))
    gath[slot(me_f, tok)] = vg_ref[...]
    wown[slot(me_s, cols)] = wt_ref[...]
    sqbuf[me_g] = sq_ref[...]

    def one_hot(n, m, start, lo, hi):
        r = lax.broadcasted_iota(jnp.int32, (n, m), 0)
        c = lax.broadcasted_iota(jnp.int32, (n, m), 1)
        hit = (c - r == start) & (r >= lo) & (r < hi)
        return jnp.where(hit, 1.0, 0.0).astype(bf16)

    def pick(n, start, lo, hi, ref):
        m = ref.shape[0]
        return jnp.dot(
            one_hot(n, m, start, lo, hi), ref[...], preferred_element_type=f32
        ).astype(bf16)

    eye = lax.broadcasted_iota(jnp.int32, (128, 128), 0) == lax.broadcasted_iota(
        jnp.int32, (128, 128), 1
    )
    for g in others_g:
        copy(sq_ref, sqbuf.at[g], s_sq.at[g], r_sq.at[g], on_g(g)).wait_recv()
    total = jnp.sum(sqbuf[...], axis=0)
    sqt_ref[...] = total
    for s in others_s:
        copy(wt_ref, wown.at[slot(s, cols)], s_w.at[s], r_w.at[s], on_s(s)).wait_recv()

    def project(k, carry):
        at = slot(k, slots)
        p = lax.dot_general(
            img_ref[at], wown[...], (((1,), (1,)), ((), ())), preferred_element_type=f32
        )
        prod[at] = p
        for j in range(0, slots, 128):
            at_j = pl.ds(pl.multiple_of(k * slots + j, 128), 128)
            inv = lax.rsqrt(sqt_ref[:, at_j] / width + epsilon)
            inv = jnp.sum(jnp.where(eye, inv, 0.0), axis=1, keepdims=True)
            part = (p[j : j + 128] * inv).astype(bf16)
            for h in range(pairs):
                pout[h, at_j] = part[:, h * half : (h + 1) * half]
        for t in others_t:
            tile_copy(t, me_t, k).start()
        return carry

    def tile_copy(t, source, k):
        at = slot(k, slots)
        return copy(
            pout.at[t, at], pin.at[source, at], s_b1.at[t, k], r_b1.at[source, k], on_t(t)
        )

    lax.fori_loop(0, tiles, project, 0)
    pin[me_t] = pout[me_t]

    for f in others_f:
        copy(vg_ref, gath.at[slot(f, tok)], s_vg.at[f], r_vg.at[f], on_f(f)).wait_recv()
    for s in others_s + [me_s]:
        block = pick(slots, a_tab[0, s], 0, a_tab[1, s], gath)
        if s is me_s:
            gin[slot(s, slots)] = block
        else:
            gout[s] = block
            send(gout.at[s], gin.at[slot(me_s, slots)], s_a2.at[s], r_a2.at[me_s], on_s(s))

    for s in others_s:
        copy(gout.at[s], gin.at[slot(s, slots)], s_a2.at[s], r_a2.at[s], on_s(s)).wait_recv()

    def order(k, carry):
        ghalf[slot(k, slots)] = pick(slots, r_tab[0, k], 0, slots, gin)
        return carry

    lax.fori_loop(0, tiles, order, 0)
    for t in others_t:
        send(ghalf, grads.at[me_t], s_a3.at[t], r_a3.at[me_t], on_t(t))
    grads[me_t] = ghalf[...]

    def arrived(k, carry):
        for t in others_t:
            tile_copy(t, t, k).wait_recv()
        return carry

    lax.fori_loop(0, tiles, arrived, 0)
    acc = pin[0].astype(f32)
    for t in range(1, pairs):
        acc = acc + pin[t].astype(f32)
    psum[...] = acc.astype(bf16)
    for s in others_s + [me_s]:
        block = pick(slots, r_tab[1, s], 0, slots, psum)
        if s is me_s:
            bin_[slot(s, slots)] = block
        else:
            bout[s] = block
            send(bout.at[s], bin_.at[slot(me_s, slots)], s_b2.at[s], r_b2.at[me_s], on_s(s))

    for t in others_t:
        copy(ghalf, grads.at[t], s_a3.at[t], r_a3.at[t], on_t(t)).wait_recv()

    def dots(k, carry):
        at = pl.ds(pl.multiple_of(k * 128, 128), 128)
        s = jnp.zeros((128, half), f32)
        for h in range(pairs):
            s = s + prod[at, h * half : (h + 1) * half] * grads[h, at].astype(f32)
        col = jnp.sum(s, axis=1, keepdims=True)
        innown[:, at] = jnp.sum(jnp.where(eye, col, 0.0), axis=0, keepdims=True)
        return carry

    lax.fori_loop(0, rows // 128, dots, 0)
    for g in others_g:
        send(innown, innbuf.at[me_g], s_in.at[g], r_in.at[me_g], on_g(g))
    innbuf[me_g] = innown[...]

    for s in others_s:
        copy(bout.at[s], bin_.at[slot(s, slots)], s_b2.at[s], r_b2.at[s], on_s(s)).wait_recv()
    for f in others_f + [me_f]:
        base = lax.rem(f * tok, slots)
        r = (f * tok) // slots
        block = pick(tok, b_tab[0, r] + base, b_tab[1, r] - base, b_tab[2, r] - base, bin_)
        if f is me_f:
            cin[f] = block
        else:
            cout[f] = block
            send(cout.at[f], cin.at[me_f], s_b3.at[f], r_b3.at[me_f], on_f(f))
    for g in others_g:
        copy(innown, innbuf.at[g], s_in.at[g], r_in.at[g], on_g(g)).wait_recv()
    inner_ref[...] = jnp.sum(innbuf[...], axis=0)
    for f in others_f:
        copy(cout.at[f], cin.at[f], s_b3.at[f], r_b3.at[f], on_f(f)).wait_recv()
    acc = cin[0].astype(f32)
    for f in range(1, columns):
        acc = acc + cin[f].astype(f32)
    vis_ref[...] = acc
    for c in sent:
        c.wait_send()

    def left(k, carry):
        for t in others_t:
            tile_copy(t, me_t, k).wait_send()
        return carry

    lax.fori_loop(0, tiles, left, 0)


def exchange(a_tab, b_tab, r_tab, vg_half, img_gain, squares, w_t, dims, width):
    sections, columns, pairs = dims
    tok, half = vg_half.shape
    rows, part = img_gain.shape
    slots = rows // r_tab.shape[1]
    heads = half * pairs
    group = columns * pairs
    vmem = pl.BlockSpec(memory_space=pltpu.VMEM)
    smem = pl.BlockSpec(memory_space=pltpu.SMEM)
    sems = []
    tiles = rows // slots
    for n in (columns, sections, group, sections, pairs, (pairs, tiles), sections, columns, group):
        sems += [pltpu.SemaphoreType.DMA(n if isinstance(n, tuple) else (n,))] * 2
    return pl.pallas_call(
        functools.partial(kernel, width),
        out_shape=(
            jax.ShapeDtypeStruct((pairs, rows, half), bf16),
            jax.ShapeDtypeStruct((tok, half), f32),
            jax.ShapeDtypeStruct((1, rows), f32),
            jax.ShapeDtypeStruct((1, rows), f32),
            jax.ShapeDtypeStruct((heads, part), bf16),
        ),
        in_specs=[smem] * 3 + [vmem] * 4,
        out_specs=(vmem,) * 5,
        scratch_shapes=[
            pltpu.VMEM((columns * tok, half), bf16),
            pltpu.VMEM((sections, slots, half), bf16),
            pltpu.VMEM((sections * slots, half), bf16),
            pltpu.VMEM((rows, half), bf16),
            pltpu.VMEM((rows, heads), f32),
            pltpu.VMEM((pairs, rows, half), bf16),
            pltpu.VMEM((pairs, rows, half), bf16),
            pltpu.VMEM((rows, half), bf16),
            pltpu.VMEM((sections, slots, half), bf16),
            pltpu.VMEM((sections * slots, half), bf16),
            pltpu.VMEM((columns, tok, half), bf16),
            pltpu.VMEM((columns, tok, half), bf16),
            pltpu.VMEM((group, 1, rows), f32),
            pltpu.VMEM((group, 1, rows), f32),
            pltpu.VMEM((1, rows), f32),
        ]
        + sems,
        compiler_params=pltpu.CompilerParams(
            collective_id=0, has_side_effects=True, vmem_limit_bytes=56 * 1024 * 1024
        ),
        cost_estimate=pl.CostEstimate(
            flops=40 * rows * part * heads, bytes_accessed=64 * rows * heads, transcendentals=0
        ),
    )(a_tab, b_tab, r_tab, vg_half, img_gain, squares, w_t)


def on_device(text_tokens, images, counts, offsets, norm_gain, value_weight, value_grad):
    sections = lax.axis_size("section")
    columns = lax.axis_size("fsdp")
    pairs = lax.axis_size("tp")
    tok_rows, width = text_tokens.shape
    tiles, slots, part = images.shape
    heads = value_grad.shape[1]
    half = heads // pairs
    group_rows = columns * tok_rows
    regions = group_rows // slots
    section = lax.axis_index("section")
    column = lax.axis_index("fsdp")
    pair = lax.axis_index("tp")

    meta = lax.all_gather(jnp.stack([offsets, counts]), "section", axis=0)
    all_off, all_cnt = meta[:, 0], meta[:, 1]
    w_all = lax.all_gather(value_weight, ("section", "fsdp"), axis=0, tiled=True)
    w_all = w_all.reshape(sections, columns * part, -1)

    here = (all_off // group_rows) == section
    start_here = jnp.sum(jnp.where(here, all_off - section * group_rows, 0), axis=1)
    count_here = jnp.sum(jnp.where(here, all_cnt, 0), axis=1)
    a_tab = jnp.stack([start_here, count_here])
    region_here = start_here // slots
    first_here = start_here % slots
    source_ids = jnp.arange(sections, dtype=jnp.int32)
    region_ids = jnp.arange(regions, dtype=jnp.int32)
    holds = region_here[None, :] == region_ids[:, None]
    by_region = jnp.stack([source_ids * slots - first_here, first_here, first_here + count_here])
    b_tab = jnp.sum(jnp.where(holds[None], by_region[:, None, :], 0), axis=2)
    target = offsets // group_rows
    tile_ids = jnp.arange(tiles, dtype=jnp.int32)
    inverse = jnp.sum(
        jnp.where(target[None, :] == source_ids[:, None], tile_ids[None, :], 0), axis=1
    )
    r_tab = jnp.stack([target, inverse]) * slots

    own = (column * pairs + pair) * part
    gain_part = lax.dynamic_slice_in_dim(norm_gain, own, part)
    flat = images.reshape(tiles * slots, part)
    flat_f = flat.astype(f32)
    img_gain = (flat_f * gain_part).astype(bf16)
    squares = jnp.sum(flat_f * flat_f, axis=1)[None, :]
    vg_half = lax.dynamic_slice_in_dim(value_grad, pair * half, half, axis=1)
    grads, visual, square_sum, inner, w_own_t = exchange(
        a_tab,
        b_tab,
        r_tab,
        vg_half,
        img_gain,
        squares,
        value_weight.T,
        (sections, columns, pairs),
        width,
    )
    first_row = column * tok_rows
    local = first_row % slots + jnp.arange(tok_rows, dtype=jnp.int32)
    bounds = lax.dynamic_index_in_dim(b_tab, first_row // slots, 1, keepdims=False)
    covered = ((local >= bounds[1]) & (local < bounds[2]))[:, None]
    text_f = text_tokens.astype(f32)
    text_rms = lax.rsqrt(jnp.sum(text_f * text_f, axis=1, keepdims=True) / width + epsilon)
    text_own = jnp.concatenate(
        [
            lax.dynamic_slice_in_dim(text_tokens, (f * pairs + pair) * part, part, axis=1)
            for f in range(columns)
        ],
        axis=1,
    )
    gain_own = jnp.concatenate(
        [
            lax.dynamic_slice_in_dim(norm_gain, (f * pairs + pair) * part, part)
            for f in range(columns)
        ]
    )
    text_gain = (text_own.astype(f32) * gain_own).astype(bf16)
    text_part = text_rms * jnp.concatenate(
        [jnp.dot(text_gain, w_all[s], preferred_element_type=f32) for s in range(sections)], axis=1
    )
    grads, text_part = lax.optimization_barrier((grads, text_part))
    text_values = lax.dynamic_slice_in_dim(text_part, pair * half, half, axis=1)
    for d in range(1, pairs):
        theirs = lax.dynamic_slice_in_dim(text_part, lax.rem(pair + d, pairs) * half, half, axis=1)
        moved = lax.ppermute(theirs.astype(bf16), "tp", [(p, (p + d) % pairs) for p in range(pairs)])
        text_values = text_values + moved.astype(f32)
    square_sum = square_sum.reshape(-1, 1)
    inner = inner.reshape(-1, 1)
    inv_rms = lax.rsqrt(square_sum / width + epsilon)
    grad_normed = sum(
        jnp.dot(grads[h], w_own_t[h * half : (h + 1) * half], preferred_element_type=f32)
        for h in range(pairs)
    )
    visual_grads = (
        inv_rms * (grad_normed * gain_part) - flat_f * (inv_rms * inv_rms * inv_rms) * inner / width
    ).astype(bf16)
    slot_ids = jnp.arange(slots, dtype=jnp.int32)
    valid = (slot_ids[None, :] < counts[:, None]).reshape(-1, 1)
    visual_grads = jnp.where(valid, visual_grads, 0).reshape(images.shape)

    values = jnp.where(covered, visual, text_values).astype(bf16)
    return (values, visual_grads)


def solution(mesh):
    placed = (
        P(("section", "fsdp"), None),
        P("section", None, ("fsdp", "tp")),
        P("section"),
        P("section"),
        P(),
        P(("fsdp", "tp"), "section"),
        P(("section", "fsdp"), None),
    )
    return jax.shard_map(
        on_device,
        mesh=mesh,
        in_specs=placed,
        out_specs=(P(("section", "fsdp"), "tp"), P("section", None, ("fsdp", "tp"))),
        check_vma=False,
    )
```

```python
import functools

import jax
import jax.numpy as jnp
from jax import lax
from jax.experimental import pallas as pl
from jax.experimental.pallas import tpu as pltpu
from jax.sharding import PartitionSpec as P

epsilon = 1e-05
f32 = jnp.float32
bf16 = jnp.bfloat16
MESH = pl.DeviceIdType.MESH


def kernel(
    width,
    a_tab,
    b_tab,
    r_tab,
    vg_ref,
    img_ref,
    sq_ref,
    wt_ref,
    grads,
    vis_ref,
    sqt_ref,
    inner_ref,
    wown,
    gath,
    gout,
    gin,
    ghalf,
    prod,
    pout,
    pin,
    psum,
    bout,
    bin_,
    cout,
    cin,
    sqbuf,
    innbuf,
    innown,
    s_vg,
    r_vg,
    s_w,
    r_w,
    s_sq,
    r_sq,
    s_a2,
    r_a2,
    s_a3,
    r_a3,
    s_b1,
    r_b1,
    s_b2,
    r_b2,
    s_b3,
    r_b3,
    s_in,
    r_in,
):
    sections, slots, half = gout.shape
    columns, tok, _ = cin.shape
    pairs = pout.shape[0]
    rows = psum.shape[0]
    tiles = rows // slots
    cols = wt_ref.shape[0]
    me_s, me_f, me_t = (lax.axis_index(n) for n in ("section", "fsdp", "tp"))
    others_s = [lax.rem(me_s + d, sections) for d in range(1, sections)]
    others_f = [lax.rem(me_f + d, columns) for d in range(1, columns)]
    others_t = [lax.rem(me_t + d, pairs) for d in range(1, pairs)]
    group = columns * pairs
    me_g = me_f * pairs + me_t
    others_g = [lax.rem(me_g + d, group) for d in range(1, group)]

    def on_s(s):
        return (s, me_f, me_t)

    def on_f(f):
        return (me_s, f, me_t)

    def on_t(t):
        return (me_s, me_f, t)

    def on_g(g):
        return (me_s, g // pairs, lax.rem(g, pairs))

    def copy(src, dst, s, r, dev):
        return pltpu.make_async_remote_copy(
            src_ref=src, dst_ref=dst, send_sem=s, recv_sem=r, device_id=dev, device_id_type=MESH
        )

    barrier = pltpu.get_barrier_semaphore()
    peers = [on_s(s) for s in others_s] + [on_g(g) for g in others_g]
    for dev in peers:
        pl.semaphore_signal(barrier, inc=1, device_id=dev, device_id_type=MESH)
    pl.semaphore_wait(barrier, len(peers))

    def slot(i, n):
        return pl.ds(pl.multiple_of(i * n, n), n)

    sent = []

    def send(src, dst, s, r, dev):
        c = copy(src, dst, s, r, dev)
        c.start()
        sent.append(c)

    for s in others_s:
        send(wt_ref, wown.at[slot(me_s, cols)], s_w.at[s], r_w.at[me_s], on_s(s))
    for g in others_g:
        send(sq_ref, sqbuf.at[me_g], s_sq.at[g], r_sq.at[me_g], on_g(g))
    for f in others_f:
        send(vg_ref, gath.at[slot(me_f, tok)], s_vg.at[f], r_vg.at[me_f], on_f(f))
    gath[slot(me_f, tok)] = vg_ref[...]
    wown[slot(me_s, cols)] = wt_ref[...]
    sqbuf[me_g] = sq_ref[...]

    def one_hot(n, m, start, lo, hi):
        r = lax.broadcasted_iota(jnp.int32, (n, m), 0)
        c = lax.broadcasted_iota(jnp.int32, (n, m), 1)
        hit = (c - r == start) & (r >= lo) & (r < hi)
        return jnp.where(hit, 1.0, 0.0).astype(bf16)

    def pick(n, start, lo, hi, ref):
        m = ref.shape[0]
        return jnp.dot(
            one_hot(n, m, start, lo, hi), ref[...], preferred_element_type=f32
        ).astype(bf16)

    def choose(start, ref):
        def step(i, acc):
            return jnp.where(start == i * slots, ref[slot(i, slots)].astype(f32), acc)

        return lax.fori_loop(0, ref.shape[0] // slots, step, jnp.zeros((slots, half), f32)).astype(
            bf16
        )

    eye = lax.broadcasted_iota(jnp.int32, (128, 128), 0) == lax.broadcasted_iota(
        jnp.int32, (128, 128), 1
    )
    for g in others_g:
        copy(sq_ref, sqbuf.at[g], s_sq.at[g], r_sq.at[g], on_g(g)).wait_recv()
    total = jnp.sum(sqbuf[...], axis=0)
    sqt_ref[...] = total
    for s in others_s:
        copy(wt_ref, wown.at[slot(s, cols)], s_w.at[s], r_w.at[s], on_s(s)).wait_recv()

    def project(k, carry):
        at = slot(k, slots)
        p = lax.dot_general(
            img_ref[at], wown[...], (((1,), (1,)), ((), ())), preferred_element_type=f32
        )
        prod[at] = p
        for j in range(0, slots, 128):
            at_j = pl.ds(pl.multiple_of(k * slots + j, 128), 128)
            inv = lax.rsqrt(sqt_ref[:, at_j] / width + epsilon)
            inv = jnp.sum(jnp.where(eye, inv, 0.0), axis=1, keepdims=True)
            part = (p[j : j + 128] * inv).astype(bf16)
            for h in range(pairs):
                pout[h, at_j] = part[:, h * half : (h + 1) * half]
        for t in others_t:
            tile_copy(t, me_t, k).start()
        return carry

    def tile_copy(t, source, k):
        at = slot(k, slots)
        return copy(
            pout.at[t, at], pin.at[source, at], s_b1.at[t, k], r_b1.at[source, k], on_t(t)
        )

    lax.fori_loop(0, tiles, project, 0)
    pin[me_t] = pout[me_t]

    for f in others_f:
        copy(vg_ref, gath.at[slot(f, tok)], s_vg.at[f], r_vg.at[f], on_f(f)).wait_recv()
    for s in others_s + [me_s]:
        block = pick(slots, a_tab[0, s], 0, a_tab[1, s], gath)
        if s is me_s:
            gin[slot(s, slots)] = block
        else:
            gout[s] = block
            send(gout.at[s], gin.at[slot(me_s, slots)], s_a2.at[s], r_a2.at[me_s], on_s(s))

    for s in others_s:
        copy(gout.at[s], gin.at[slot(s, slots)], s_a2.at[s], r_a2.at[s], on_s(s)).wait_recv()

    def order(k, carry):
        ghalf[slot(k, slots)] = choose(r_tab[0, k], gin)
        return carry

    lax.fori_loop(0, tiles, order, 0)
    for t in others_t:
        send(ghalf, grads.at[me_t], s_a3.at[t], r_a3.at[me_t], on_t(t))
    grads[me_t] = ghalf[...]

    def arrived(k, carry):
        for t in others_t:
            tile_copy(t, t, k).wait_recv()
        return carry

    lax.fori_loop(0, tiles, arrived, 0)
    acc = pin[0].astype(f32)
    for t in range(1, pairs):
        acc = acc + pin[t].astype(f32)
    psum[...] = acc.astype(bf16)
    for s in others_s + [me_s]:
        block = choose(r_tab[1, s], psum)
        if s is me_s:
            bin_[slot(s, slots)] = block
        else:
            bout[s] = block
            send(bout.at[s], bin_.at[slot(me_s, slots)], s_b2.at[s], r_b2.at[me_s], on_s(s))

    for t in others_t:
        copy(ghalf, grads.at[t], s_a3.at[t], r_a3.at[t], on_t(t)).wait_recv()

    def dots(k, carry):
        at = pl.ds(pl.multiple_of(k * 128, 128), 128)
        s = jnp.zeros((128, half), f32)
        for h in range(pairs):
            s = s + prod[at, h * half : (h + 1) * half] * grads[h, at].astype(f32)
        col = jnp.sum(s, axis=1, keepdims=True)
        innown[:, at] = jnp.sum(jnp.where(eye, col, 0.0), axis=0, keepdims=True)
        return carry

    lax.fori_loop(0, rows // 128, dots, 0)
    for g in others_g:
        send(innown, innbuf.at[me_g], s_in.at[g], r_in.at[me_g], on_g(g))
    innbuf[me_g] = innown[...]

    for s in others_s:
        copy(bout.at[s], bin_.at[slot(s, slots)], s_b2.at[s], r_b2.at[s], on_s(s)).wait_recv()
    for f in others_f + [me_f]:
        base = lax.rem(f * tok, slots)
        r = (f * tok) // slots
        block = pick(tok, b_tab[0, r] + base, b_tab[1, r] - base, b_tab[2, r] - base, bin_)
        if f is me_f:
            cin[f] = block
        else:
            cout[f] = block
            send(cout.at[f], cin.at[me_f], s_b3.at[f], r_b3.at[me_f], on_f(f))
    for g in others_g:
        copy(innown, innbuf.at[g], s_in.at[g], r_in.at[g], on_g(g)).wait_recv()
    inner_ref[...] = jnp.sum(innbuf[...], axis=0)
    for f in others_f:
        copy(cout.at[f], cin.at[f], s_b3.at[f], r_b3.at[f], on_f(f)).wait_recv()
    acc = cin[0].astype(f32)
    for f in range(1, columns):
        acc = acc + cin[f].astype(f32)
    vis_ref[...] = acc
    for c in sent:
        c.wait_send()

    def left(k, carry):
        for t in others_t:
            tile_copy(t, me_t, k).wait_send()
        return carry

    lax.fori_loop(0, tiles, left, 0)


def exchange(a_tab, b_tab, r_tab, vg_half, img_gain, squares, w_t, dims, width):
    sections, columns, pairs = dims
    tok, half = vg_half.shape
    rows, part = img_gain.shape
    slots = rows // r_tab.shape[1]
    heads = half * pairs
    group = columns * pairs
    vmem = pl.BlockSpec(memory_space=pltpu.VMEM)
    smem = pl.BlockSpec(memory_space=pltpu.SMEM)
    sems = []
    tiles = rows // slots
    for n in (columns, sections, group, sections, pairs, (pairs, tiles), sections, columns, group):
        sems += [pltpu.SemaphoreType.DMA(n if isinstance(n, tuple) else (n,))] * 2
    return pl.pallas_call(
        functools.partial(kernel, width),
        out_shape=(
            jax.ShapeDtypeStruct((pairs, rows, half), bf16),
            jax.ShapeDtypeStruct((tok, half), f32),
            jax.ShapeDtypeStruct((1, rows), f32),
            jax.ShapeDtypeStruct((1, rows), f32),
            jax.ShapeDtypeStruct((heads, part), bf16),
        ),
        in_specs=[smem] * 3 + [vmem] * 4,
        out_specs=(vmem,) * 5,
        scratch_shapes=[
            pltpu.VMEM((columns * tok, half), bf16),
            pltpu.VMEM((sections, slots, half), bf16),
            pltpu.VMEM((sections * slots, half), bf16),
            pltpu.VMEM((rows, half), bf16),
            pltpu.VMEM((rows, heads), f32),
            pltpu.VMEM((pairs, rows, half), bf16),
            pltpu.VMEM((pairs, rows, half), bf16),
            pltpu.VMEM((rows, half), bf16),
            pltpu.VMEM((sections, slots, half), bf16),
            pltpu.VMEM((sections * slots, half), bf16),
            pltpu.VMEM((columns, tok, half), bf16),
            pltpu.VMEM((columns, tok, half), bf16),
            pltpu.VMEM((group, 1, rows), f32),
            pltpu.VMEM((group, 1, rows), f32),
            pltpu.VMEM((1, rows), f32),
        ]
        + sems,
        compiler_params=pltpu.CompilerParams(
            collective_id=0, has_side_effects=True, vmem_limit_bytes=56 * 1024 * 1024
        ),
        cost_estimate=pl.CostEstimate(
            flops=40 * rows * part * heads, bytes_accessed=64 * rows * heads, transcendentals=0
        ),
    )(a_tab, b_tab, r_tab, vg_half, img_gain, squares, w_t)


def on_device(text_tokens, images, counts, offsets, norm_gain, value_weight, value_grad):
    sections = lax.axis_size("section")
    columns = lax.axis_size("fsdp")
    pairs = lax.axis_size("tp")
    tok_rows, width = text_tokens.shape
    tiles, slots, part = images.shape
    heads = value_grad.shape[1]
    half = heads // pairs
    group_rows = columns * tok_rows
    regions = group_rows // slots
    section = lax.axis_index("section")
    column = lax.axis_index("fsdp")
    pair = lax.axis_index("tp")

    meta = lax.all_gather(jnp.stack([offsets, counts]), "section", axis=0)
    all_off, all_cnt = meta[:, 0], meta[:, 1]
    w_all = lax.all_gather(value_weight, ("section", "fsdp"), axis=0, tiled=True)
    w_all = w_all.reshape(sections, columns * part, -1)

    here = (all_off // group_rows) == section
    start_here = jnp.sum(jnp.where(here, all_off - section * group_rows, 0), axis=1)
    count_here = jnp.sum(jnp.where(here, all_cnt, 0), axis=1)
    a_tab = jnp.stack([start_here, count_here])
    region_here = start_here // slots
    first_here = start_here % slots
    source_ids = jnp.arange(sections, dtype=jnp.int32)
    region_ids = jnp.arange(regions, dtype=jnp.int32)
    holds = region_here[None, :] == region_ids[:, None]
    by_region = jnp.stack([source_ids * slots - first_here, first_here, first_here + count_here])
    b_tab = jnp.sum(jnp.where(holds[None], by_region[:, None, :], 0), axis=2)
    target = offsets // group_rows
    tile_ids = jnp.arange(tiles, dtype=jnp.int32)
    inverse = jnp.sum(
        jnp.where(target[None, :] == source_ids[:, None], tile_ids[None, :], 0), axis=1
    )
    r_tab = jnp.stack([target, inverse]) * slots

    own = (column * pairs + pair) * part
    gain_part = lax.dynamic_slice_in_dim(norm_gain, own, part)
    flat = images.reshape(tiles * slots, part)
    flat_f = flat.astype(f32)
    img_gain = (flat_f * gain_part).astype(bf16)
    squares = jnp.sum(flat_f * flat_f, axis=1)[None, :]
    vg_half = lax.dynamic_slice_in_dim(value_grad, pair * half, half, axis=1)
    grads, visual, square_sum, inner, w_own_t = exchange(
        a_tab,
        b_tab,
        r_tab,
        vg_half,
        img_gain,
        squares,
        value_weight.T,
        (sections, columns, pairs),
        width,
    )
    first_row = column * tok_rows
    local = first_row % slots + jnp.arange(tok_rows, dtype=jnp.int32)
    bounds = lax.dynamic_index_in_dim(b_tab, first_row // slots, 1, keepdims=False)
    covered = ((local >= bounds[1]) & (local < bounds[2]))[:, None]
    text_f = text_tokens.astype(f32)
    text_rms = lax.rsqrt(jnp.sum(text_f * text_f, axis=1, keepdims=True) / width + epsilon)
    text_own = jnp.concatenate(
        [
            lax.dynamic_slice_in_dim(text_tokens, (f * pairs + pair) * part, part, axis=1)
            for f in range(columns)
        ],
        axis=1,
    )
    gain_own = jnp.concatenate(
        [
            lax.dynamic_slice_in_dim(norm_gain, (f * pairs + pair) * part, part)
            for f in range(columns)
        ]
    )
    text_gain = (text_own.astype(f32) * gain_own).astype(bf16)
    text_part = text_rms * jnp.concatenate(
        [jnp.dot(text_gain, w_all[s], preferred_element_type=f32) for s in range(sections)], axis=1
    )
    grads, text_part = lax.optimization_barrier((grads, text_part))
    text_values = lax.dynamic_slice_in_dim(text_part, pair * half, half, axis=1)
    for d in range(1, pairs):
        theirs = lax.dynamic_slice_in_dim(text_part, lax.rem(pair + d, pairs) * half, half, axis=1)
        moved = lax.ppermute(theirs.astype(bf16), "tp", [(p, (p + d) % pairs) for p in range(pairs)])
        text_values = text_values + moved.astype(f32)
    square_sum = square_sum.reshape(-1, 1)
    inner = inner.reshape(-1, 1)
    inv_rms = lax.rsqrt(square_sum / width + epsilon)
    grad_normed = sum(
        jnp.dot(grads[h], w_own_t[h * half : (h + 1) * half], preferred_element_type=f32)
        for h in range(pairs)
    )
    visual_grads = (
        inv_rms * (grad_normed * gain_part) - flat_f * (inv_rms * inv_rms * inv_rms) * inner / width
    ).astype(bf16)
    slot_ids = jnp.arange(slots, dtype=jnp.int32)
    valid = (slot_ids[None, :] < counts[:, None]).reshape(-1, 1)
    visual_grads = jnp.where(valid, visual_grads, 0).reshape(images.shape)

    values = jnp.where(covered, visual, text_values).astype(bf16)
    return (values, visual_grads)


def solution(mesh):
    placed = (
        P(("section", "fsdp"), None),
        P("section", None, ("fsdp", "tp")),
        P("section"),
        P("section"),
        P(),
        P(("fsdp", "tp"), "section"),
        P(("section", "fsdp"), None),
    )
    return jax.shard_map(
        on_device,
        mesh=mesh,
        in_specs=placed,
        out_specs=(P(("section", "fsdp"), "tp"), P("section", None, ("fsdp", "tp"))),
        check_vma=False,
    )
```
